32 devices in a mesh: section: 16 (over z, x, core), team: 2 (over y).
Axes of the slice: x: 2, y: 2, z: 4, core: 2. Of those that a mesh axis runs over, the one named last changes fastest.
Arguments:
- amps: bfloat16 [1024, 8192], P('team', 'section'), may hold values from -6 to 6
- t_mask: int32 [8, 64], P('team', 'section'), may hold values from 0 to 1, as said below
- ints: bfloat16 [8192, 8192], P('team', 'section'), may hold values from -0.09375 to 0.09375
- v_mask: int32 [64, 64], P('team', 'section'), may hold values 0 or 1
Outputs:
- ladder: bfloat16 [1024, 8192], P('team', 'section')
The draws below stay inside these ranges and needn't reach their ends.
Inputs may be any that keep to these rules, and one draw needn't show every extreme that they name: `t_mask`: in every row of tiles, each aligned group of 4 tile columns holds exactly 2 ones; which ones is random.
All inputs are finite; a program needn't handle non-finite values. No bound on the sum of `v_mask` on one device may be relied on, other than what follows from the above.
Results may differ from the reference program's by a relative error of at most 0.001.
Values may be sent and summed in bfloat16 or wider, within the bound.
A program may use at most 128 MiB of HBM per device.

```python
import jax
import jax.numpy as jnp
from jax import lax

TILE = 128
PANEL_TILES = 4
NZ = 2
OCC_DEV = 512
VP = 8192
OCC = 1024
AB = 8192


def draw_t_mask(key, part):
    row_tiles = OCC // TILE
    groups = VP // (PANEL_TILES * TILE)
    scores = jax.random.randint(key, (row_tiles, groups, PANEL_TILES), 0, 1 << 20)
    scores = scores * PANEL_TILES + jnp.arange(PANEL_TILES, dtype=jnp.int32)
    order = jnp.argsort(scores, axis=2, stable=True)
    ranks = jnp.argsort(order, axis=2, stable=True)
    chosen = (ranks < NZ).astype(jnp.int32)
    return chosen.reshape(row_tiles, groups * PANEL_TILES)


def set_ends(array, key, low, high):
    spot = [jax.random.randint(jax.random.fold_in(key, axis), (), 0, length) for axis, length in enumerate(array.shape)]
    longest = array.shape.index(max(array.shape))
    next_to = spot[:longest] + [(spot[longest] + 1) % array.shape[longest]] + spot[longest + 1:]
    return array.at[tuple(spot)].set(low).at[tuple(next_to)].set(high)


def levels(own_key, shape, shards, low, top_value):
    loudness = 1.0
    for dim, parts in shards:
        steps = jax.random.uniform(jax.random.fold_in(jax.random.fold_in(own_key, 6), dim), (parts,), jnp.float32, low / len(shards), top_value / len(shards))
        loudness = loudness * jnp.repeat(jnp.exp(steps), shape[dim] // parts).reshape((-1,) + (1,) * (len(shape) - 1 - dim))
    return loudness


def bell_draw(key, extent, deviation, reach, split=(), kind=jnp.bfloat16):
    entries = deviation * jax.random.normal(key, extent, jnp.float32)
    if split:
        entries = entries * levels(key, extent, split, -0.22, 0.18)
    return jnp.clip(entries, -reach, reach).astype(kind)


def setup_inputs(seed: int = 0) -> dict:
    splits = jax.random.split(jax.random.key(seed), 5)
    amps = bell_draw(splits[0], (OCC, VP), 1.0, 6.0, ((0, 2), (1, 16)))
    t_mask = draw_t_mask(jax.random.fold_in(splits[4], 71), 0)
    ints = bell_draw(splits[2], (VP, AB), (VP // 2) ** -0.5, 0.09375, ((0, 2), (1, 16)))
    v_mask = set_ends((jax.random.randint(splits[3], (VP // TILE, AB // TILE), 0, 4) < 3).astype(jnp.int32), jax.random.fold_in(splits[3], 1), 0, 1)
    return {"amps": amps, "t_mask": t_mask, "ints": ints, "v_mask": v_mask}


def expand_mask(values, mask):
    rows, cols = values.shape
    tiles = values.reshape(rows // TILE, TILE, cols // TILE, TILE)
    scaled = tiles * mask.astype(values.dtype)[:, None, :, None]
    return scaled.reshape(rows, cols)


def reference(amps, t_mask, ints, v_mask):
    t_eff = expand_mask(amps, t_mask)
    v_eff = expand_mask(ints, v_mask)
    blocks = t_eff.reshape(OCC // OCC_DEV, OCC_DEV, VP)

    def one_block(block):
        return jnp.dot(block, v_eff, preferred_element_type=jnp.float32).astype(jnp.bfloat16)

    result = lax.map(one_block, blocks)
    return result.reshape(OCC, AB)
```

```python
import functools

import jax
import jax.numpy as jnp
from jax import lax
from jax.experimental import pallas as pl
from jax.experimental.pallas import tpu as pltpu
from jax.sharding import PartitionSpec as P

TILE = 128
NZ = 2
CORES = 2
MESH = pl.DeviceIdType.MESH


def kernel(sections, teams, columns, amps_ref, tm_ref, vm_ref, ints_ref, out_ref,
           mine, buf, v, texp, acc, part, got, load_sem, y_sem, send_sem, recv_sem, part_sem, got_sem):
    rows, panel = amps_ref.shape
    row_tiles, tiles = rows // TILE, panel // TILE
    share = sections // teams
    levels = sections // (CORES * columns)
    s, t = lax.axis_index("section"), lax.axis_index("team")
    core, chip = lax.rem(s, CORES), lax.div(s, CORES)
    x, z = lax.rem(chip, columns), lax.div(chip, columns)
    group = lax.div(s, share)
    sibling = s + 1 - 2 * core

    def at(section, team):
        return {"section": section, "team": team}

    load = pltpu.make_async_copy(ints_ref, v, load_sem)
    load.start()

    barrier = pltpu.get_barrier_semaphore()

    def greet(section, team):
        pl.semaphore_signal(barrier, inc=1, device_id=at(section, team), device_id_type=MESH)

    greet(sibling, t)
    for d in range(1, columns):
        greet(s + CORES * (lax.rem(x + d, columns) - x), t)
    for d in range(1, teams):
        greet(s, lax.rem(t + d, teams))
    step = CORES * columns

    @pl.when(z > 0)
    def _():
        greet(s - step, t)

    @pl.when(z < levels - 1)
    def _():
        greet(s + step, t)

    partners = 1 + (columns - 1) + (teams - 1)
    partners = partners + jnp.where(z > 0, 1, 0) + jnp.where(z < levels - 1, 1, 0)

    shape = (row_tiles * tiles, NZ * TILE)
    table_row = lax.broadcasted_iota(jnp.int32, shape, 0)
    table_lane = lax.broadcasted_iota(jnp.int32, shape, 1)
    hits = jnp.zeros(shape, jnp.float32)
    for i in range(row_tiles):
        before = jnp.int32(0)
        for c in range(tiles):
            one = tm_ref[i, c]
            for j in range(NZ):
                hit = jnp.where(before == j, one, 0).astype(jnp.float32)
                place = (table_row == i * tiles + c) & (table_lane >= j * TILE) & (table_lane < (j + 1) * TILE)
                hits = jnp.where(place, hit, hits)
            before = before + one

    def spread(table, i, c, j):
        row = table[i * tiles + c : i * tiles + c + 1, j * TILE : (j + 1) * TILE]
        return jnp.broadcast_to(row.astype(jnp.bfloat16), (TILE, TILE))

    for i in range(row_tiles):
        for j in range(NZ):
            total = None
            for c in range(tiles):
                tile = amps_ref[i * TILE : (i + 1) * TILE, c * TILE : (c + 1) * TILE]
                term = tile * spread(hits, i, c, j)
                total = term if total is None else total + term
            mine[i * TILE : (i + 1) * TILE, j * TILE : (j + 1) * TILE] = total
    mine[rows:, :] = hits.astype(jnp.bfloat16)
    own = t * share + lax.rem(s, share)

    @pl.when(group == t)
    def _():
        buf[own] = mine[...]

    pl.semaphore_wait(barrier, partners)

    def y_copy():
        return pltpu.make_async_remote_copy(
            src_ref=mine, dst_ref=buf.at[own], send_sem=y_sem, recv_sem=recv_sem.at[own],
            device_id=at(s, group), device_id_type=MESH)

    @pl.when(group != t)
    def _():
        y_copy().start()

    def slot(n):
        i, u = lax.div(n, share), lax.rem(n, share)
        source = lax.rem(t + 1 + i, teams)
        return source, u, source * share + u, t * share + u

    def forward(n, go):
        source, u, k, home = slot(n)
        home_core, home_chip = lax.rem(home, CORES), lax.div(home, CORES)
        home_x, home_z = lax.rem(home_chip, columns), lax.div(home_chip, columns)
        straight = core == home_core
        column = straight & (x == home_x)

        def copy(kind, section):
            return pltpu.make_async_remote_copy(
                src_ref=buf.at[k], dst_ref=buf.at[k], send_sem=send_sem.at[kind, k], recv_sem=recv_sem.at[k],
                device_id=at(section, t), device_id_type=MESH)

        @pl.when(column & (z >= home_z) & (z < levels - 1))
        def _():
            go(copy(0, s + step))

        @pl.when(column & (z <= home_z) & (z > 0))
        def _():
            go(copy(1, s - step))

        for d in range(1, columns):
            @pl.when(column)
            def _():
                go(copy(2 + d, s + CORES * (lax.rem(x + d, columns) - x)))

        @pl.when(straight)
        def _():
            go(copy(2, sibling))

    def arrive(n):
        source, u, k, home = slot(n)

        @pl.when((s != home) | (source != t))
        def _():
            pltpu.make_async_remote_copy(
                src_ref=buf.at[k], dst_ref=buf.at[k], send_sem=send_sem.at[2, k], recv_sem=recv_sem.at[k],
                device_id=at(sibling, t), device_id_type=MESH).wait_recv()

    load.wait()

    @pl.loop(0, v.shape[0] // TILE)
    def _(k):
        here = pl.ds(pl.multiple_of(k * TILE, TILE), TILE)
        for c in range(v.shape[1] // TILE):
            lanes = slice(c * TILE, (c + 1) * TILE)
            v[here, lanes] = v[here, lanes] * jnp.full((TILE, TILE), vm_ref[k, c].astype(jnp.float32)).astype(jnp.bfloat16)

    def part_copy(d):
        return pltpu.make_async_remote_copy(
            src_ref=part.at[d - 1], dst_ref=got.at[teams - d - 1], send_sem=part_sem.at[d - 1],
            recv_sem=got_sem.at[teams - d - 1], device_id=at(s, lax.rem(t + d, teams)), device_id_type=MESH)

    def one_team(d):
        acc[...] = jnp.zeros_like(acc)

        @pl.loop(0, share)
        def _(u):
            n = (d - 1) * share + u
            arrive(n)
            forward(n, lambda copy: copy.start())
            _, _, k, _ = slot(n)
            table = buf[k, rows:, :].astype(jnp.float32)
            for i in range(row_tiles):
                for c in range(tiles):
                    tile = None
                    for j in range(NZ):
                        term = buf[k, i * TILE : (i + 1) * TILE, j * TILE : (j + 1) * TILE] * spread(table, i, c, j)
                        tile = term if tile is None else tile + term
                    texp[i * TILE : (i + 1) * TILE, c * TILE : (c + 1) * TILE] = tile
            here = pl.ds(pl.multiple_of(u * panel, panel), panel)
            acc[...] += jnp.dot(texp[...], v[here, :], preferred_element_type=jnp.float32)

    for d in range(1, teams):
        one_team(d)
        part[d - 1] = acc[...]
        part_copy(d).start()
    one_team(teams)
    for d in range(1, teams):
        part_copy(d).wait_recv()
        acc[...] += got[teams - d - 1]
    out_ref[...] = acc[...].astype(out_ref.dtype)

    @pl.when(group != t)
    def _():
        y_copy().wait_send()

    @pl.loop(0, teams * share)
    def _(n):
        forward(n, lambda copy: copy.wait_send())

    for d in range(1, teams):
        part_copy(d).wait_send()


def shards(sections, teams, columns, amps, t_mask, ints, v_mask):
    rows, panel = amps.shape
    depth, ab_cols = ints.shape
    slots = sections
    message = (rows + t_mask.shape[0] * t_mask.shape[1], NZ * TILE)
    smem = pl.BlockSpec(memory_space=pltpu.SMEM)
    vmem = pl.BlockSpec(memory_space=pltpu.VMEM)
    return pl.pallas_call(
        functools.partial(kernel, sections, teams, columns),
        out_shape=jax.ShapeDtypeStruct((rows, ab_cols), jnp.bfloat16),
        in_specs=[vmem, smem, smem, pl.BlockSpec(memory_space=pl.ANY)],
        out_specs=vmem,
        scratch_shapes=[
            pltpu.VMEM(message, jnp.bfloat16),
            pltpu.VMEM((slots, *message), jnp.bfloat16),
            pltpu.VMEM((depth, ab_cols), jnp.bfloat16),
            pltpu.VMEM((rows, panel), jnp.bfloat16),
            pltpu.VMEM((rows, ab_cols), jnp.float32),
            pltpu.VMEM((teams - 1, rows, ab_cols), jnp.float32),
            pltpu.VMEM((teams - 1, rows, ab_cols), jnp.float32),
            pltpu.SemaphoreType.DMA,
            pltpu.SemaphoreType.DMA,
            pltpu.SemaphoreType.DMA((2 + columns, slots)),
            pltpu.SemaphoreType.DMA((slots,)),
            pltpu.SemaphoreType.DMA((teams - 1,)),
            pltpu.SemaphoreType.DMA((teams - 1,)),
        ],
        compiler_params=pltpu.CompilerParams(
            collective_id=0, has_side_effects=True, vmem_limit_bytes=48 * 2**20
        ),
        cost_estimate=pl.CostEstimate(
            flops=2 * teams * rows * depth * ab_cols, bytes_accessed=2 * depth * ab_cols, transcendentals=0
        ),
    )(amps, t_mask, v_mask, ints)


def solution(mesh):
    sections, teams = mesh.shape["section"], mesh.shape["team"]
    chips = sections // CORES
    columns = 1
    while (2 * columns) ** 2 <= chips and chips % (2 * columns) == 0:
        columns *= 2
    spec = P("team", "section")
    return jax.shard_map(
        functools.partial(shards, sections, teams, columns),
        mesh=mesh, in_specs=(spec,) * 4, out_specs=spec, check_vma=False)
```

```python
import functools

import jax
import jax.numpy as jnp
from jax import lax
from jax.experimental import pallas as pl
from jax.experimental.pallas import tpu as pltpu
from jax.sharding import PartitionSpec as P

TILE = 128
NZ = 2
CORES = 2
MESH = pl.DeviceIdType.MESH


def kernel(sections, teams, columns, amps_ref, tm_ref, vm_ref, ints_ref, out_ref,
           mine, buf, v, texp, acc, part, got, load_sem, y_sem, send_sem, recv_sem, part_sem, got_sem):
    pieces, rows = mine.shape[0], texp.shape[0]
    panel = amps_ref.shape[1]
    row_tiles, tiles = rows // TILE, panel // TILE
    share = sections // teams
    levels = sections // (CORES * columns)
    step = CORES * columns
    width = min(share, step)
    depth, span = share // width, width // CORES
    s, t = lax.axis_index("section"), lax.axis_index("team")
    core, chip = lax.rem(s, CORES), lax.div(s, CORES)
    x, z = lax.rem(chip, columns), lax.div(chip, columns)
    group = lax.div(s, share)
    sibling = s + 1 - 2 * core
    first, offset = lax.div(t * share, step), lax.rem(t * share, step)

    def at(section, team):
        return {"section": section, "team": team}

    load = pltpu.make_async_copy(ints_ref, v, load_sem)
    load.start()

    barrier = pltpu.get_barrier_semaphore()

    def greet(section, team):
        pl.semaphore_signal(barrier, inc=1, device_id=at(section, team), device_id_type=MESH)

    greet(sibling, t)
    for d in range(1, columns):
        greet(s + CORES * (lax.rem(x + d, columns) - x), t)
    for d in range(1, teams):
        greet(s, lax.rem(t + d, teams))

    @pl.when(z > 0)
    def _():
        greet(s - step, t)

    @pl.when(z < levels - 1)
    def _():
        greet(s + step, t)

    partners = 1 + (columns - 1) + (teams - 1)
    partners = partners + jnp.where(z > 0, 1, 0) + jnp.where(z < levels - 1, 1, 0)

    def spread(table, i, c, j):
        row = table[i * tiles + c : i * tiles + c + 1, j * TILE : (j + 1) * TILE]
        return jnp.broadcast_to(row.astype(jnp.bfloat16), (TILE, TILE))

    shape = (mine.shape[1] - rows, NZ * TILE)
    table_row = lax.broadcasted_iota(jnp.int32, shape, 0)
    table_lane = lax.broadcasted_iota(jnp.int32, shape, 1)
    for h in range(pieces):
        hits = jnp.zeros(shape, jnp.float32)
        for i in range(row_tiles):
            before = jnp.int32(0)
            for c in range(tiles):
                one = tm_ref[h * row_tiles + i, c]
                for j in range(NZ):
                    hit = jnp.where(before == j, one, 0).astype(jnp.float32)
                    place = (table_row == i * tiles + c) & (table_lane >= j * TILE) & (table_lane < (j + 1) * TILE)
                    hits = jnp.where(place, hit, hits)
                before = before + one
        for i in range(row_tiles):
            r = (h * row_tiles + i) * TILE
            for j in range(NZ):
                total = None
                for c in range(tiles):
                    term = amps_ref[r : r + TILE, c * TILE : (c + 1) * TILE] * spread(hits, i, c, j)
                    total = term if total is None else total + term
                mine[h, i * TILE : (i + 1) * TILE, j * TILE : (j + 1) * TILE] = total
        mine[h, rows:, :] = hits.astype(jnp.bfloat16)

    def place_of(h, source, home):
        return (h * teams + source) * share + home

    def own(h):
        return place_of(h, t, lax.rem(s, share))

    @pl.when(group == t)
    def _():
        for h in range(pieces):
            buf[own(h)] = mine[h]

    pl.semaphore_wait(barrier, partners)

    def y_copy(h):
        return pltpu.make_async_remote_copy(
            src_ref=mine.at[h], dst_ref=buf.at[own(h)], send_sem=y_sem.at[h], recv_sem=recv_sem.at[own(h)],
            device_id=at(s, group), device_id_type=MESH)

    @pl.when(group != t)
    def _():
        for h in range(pieces):
            y_copy(h).start()

    phases = teams * pieces

    def slot(p, level, w):
        source = lax.rem(t + 1 + lax.div(p, pieces), teams)
        up, down = first + level, first + depth - 1 - level
        turn = first + lax.rem(z - first + level + depth, depth)
        row = jnp.where(z <= first, up, jnp.where(z >= first + depth - 1, down, turn))
        far = lax.rem(x + w, span)
        side = lax.rem(core + lax.div(w, span), CORES)
        home = row * step + offset + CORES * far + side
        u = home - t * share
        return source, u, place_of(lax.rem(p, pieces), source, u), home

    def relay(k, home, go):
        home_core, home_chip = lax.rem(home, CORES), lax.div(home, CORES)
        home_x, home_z = lax.rem(home_chip, columns), lax.div(home_chip, columns)
        straight = core == home_core
        column = straight & (x == home_x)

        def copy(kind, section):
            return pltpu.make_async_remote_copy(
                src_ref=buf.at[k], dst_ref=buf.at[k], send_sem=send_sem.at[kind, k], recv_sem=recv_sem.at[k],
                device_id=at(section, t), device_id_type=MESH)

        @pl.when(column & (z >= home_z) & (z < levels - 1))
        def _():
            go(copy(0, s + step))

        @pl.when(column & (z <= home_z) & (z > 0))
        def _():
            go(copy(1, s - step))

        for d in range(1, columns):
            @pl.when(column)
            def _():
                go(copy(2 + d, s + CORES * (lax.rem(x + d, columns) - x)))

        @pl.when(straight)
        def _():
            go(copy(2, sibling))

    def arrive(k, home, source):
        @pl.when((s != home) | (source != t))
        def _():
            pltpu.make_async_remote_copy(
                src_ref=buf.at[k], dst_ref=buf.at[k], send_sem=send_sem.at[2, k], recv_sem=recv_sem.at[k],
                device_id=at(sibling, t), device_id_type=MESH).wait_recv()

    def pass_on(p, level, w):
        source, _, k, home = slot(p, level, w)
        arrive(k, home, source)
        relay(k, home, lambda copy: copy.start())

    @pl.when(group == t)
    def _():
        for h in range(pieces):
            relay(own(h), s, lambda copy: copy.start())

    load.wait()

    @pl.loop(0, v.shape[0] // TILE)
    def _(k):
        here = pl.ds(pl.multiple_of(k * TILE, TILE), TILE)
        for c in range(v.shape[1] // TILE):
            lanes = slice(c * TILE, (c + 1) * TILE)
            v[here, lanes] = v[here, lanes] * jnp.full((TILE, TILE), vm_ref[k, c].astype(jnp.float32)).astype(jnp.bfloat16)

    def part_copy(p):
        d, h = p // pieces + 1, p % pieces
        there = (teams - d - 1) * pieces + h
        return pltpu.make_async_remote_copy(
            src_ref=part.at[p], dst_ref=got.at[there], send_sem=part_sem.at[p],
            recv_sem=got_sem.at[there], device_id=at(s, lax.rem(t + d, teams)), device_id_type=MESH)

    def columns_of(p):
        for level in range(1 if p >= phases - pieces else 0, depth):
            pass_on(p, level, 0)

    def rest_of(p):
        for level in range(depth):
            for w in range(1, span):
                pass_on(p, level, w)

    def compute(p):
        acc[...] = jnp.zeros_like(acc)

        @pl.loop(0, share)
        def _(n):
            level, w = lax.div(n, width), lax.rem(n, width)
            source, u, k, home = slot(p, level, w)

            @pl.when(w >= span)
            def _():
                arrive(k, home, source)

            table = buf[k, rows:, :].astype(jnp.float32)
            for i in range(row_tiles):
                for c in range(tiles):
                    tile = None
                    for j in range(NZ):
                        term = buf[k, i * TILE : (i + 1) * TILE, j * TILE : (j + 1) * TILE] * spread(table, i, c, j)
                        tile = term if tile is None else tile + term
                    texp[i * TILE : (i + 1) * TILE, c * TILE : (c + 1) * TILE] = tile
            here = pl.ds(pl.multiple_of(u * panel, panel), panel)
            acc[...] += jnp.dot(texp[...], v[here, :], preferred_element_type=jnp.float32)

    for p in range(phases - pieces, phases):
        source, _, k, home = slot(p, 0, 0)

        @pl.when(s != home)
        def _():
            pass_on(p, 0, 0)

    columns_of(0)
    for p in range(phases):
        if p + 1 < phases:
            columns_of(p + 1)
        rest_of(p)
        compute(p)
        if p < phases - pieces:
            part[p] = acc[...]
            part_copy(p).start()
        else:
            h = p - (phases - pieces)
            for d in range(1, teams):
                there = (d - 1) * pieces + h
                part_copy((teams - d - 1) * pieces + h).wait_recv()
                acc[...] += got[there]
            out_ref[h * rows : (h + 1) * rows, :] = acc[...].astype(out_ref.dtype)

    @pl.when(group != t)
    def _():
        for h in range(pieces):
            y_copy(h).wait_send()

    @pl.loop(0, phases * share)
    def _(n):
        p, n = lax.div(n, share), lax.rem(n, share)
        _, _, k, home = slot(p, lax.div(n, width), lax.rem(n, width))
        relay(k, home, lambda copy: copy.wait_send())

    for p in range(phases - pieces):
        part_copy(p).wait_send()


def shards(sections, teams, columns, amps, t_mask, ints, v_mask):
    rows, panel = amps.shape
    depth, ab_cols = ints.shape
    row_tiles = rows // TILE
    pieces = 2 if row_tiles % 2 == 0 else 1
    piece = rows // pieces
    table = t_mask.shape[0] * t_mask.shape[1] // pieces
    message = (piece + -(-table // 16) * 16, NZ * TILE)
    slots, parts = pieces * sections, pieces * (teams - 1)
    smem = pl.BlockSpec(memory_space=pltpu.SMEM)
    vmem = pl.BlockSpec(memory_space=pltpu.VMEM)
    return pl.pallas_call(
        functools.partial(kernel, sections, teams, columns),
        out_shape=jax.ShapeDtypeStruct((rows, ab_cols), jnp.bfloat16),
        in_specs=[vmem, smem, smem, pl.BlockSpec(memory_space=pl.ANY)],
        out_specs=vmem,
        scratch_shapes=[
            pltpu.VMEM((pieces, *message), jnp.bfloat16),
            pltpu.VMEM((slots, *message), jnp.bfloat16),
            pltpu.VMEM((depth, ab_cols), jnp.bfloat16),
            pltpu.VMEM((piece, panel), jnp.bfloat16),
            pltpu.VMEM((piece, ab_cols), jnp.float32),
            pltpu.VMEM((parts, piece, ab_cols), jnp.float32),
            pltpu.VMEM((parts, piece, ab_cols), jnp.float32),
            pltpu.SemaphoreType.DMA,
            pltpu.SemaphoreType.DMA((pieces,)),
            pltpu.SemaphoreType.DMA((2 + columns, slots)),
            pltpu.SemaphoreType.DMA((slots,)),
            pltpu.SemaphoreType.DMA((parts,)),
            pltpu.SemaphoreType.DMA((parts,)),
        ],
        compiler_params=pltpu.CompilerParams(
            collective_id=0, has_side_effects=True, vmem_limit_bytes=48 * 2**20
        ),
        cost_estimate=pl.CostEstimate(
            flops=2 * teams * rows * depth * ab_cols, bytes_accessed=2 * depth * ab_cols, transcendentals=0
        ),
    )(amps, t_mask, v_mask, ints)


def solution(mesh):
    sections, teams = mesh.shape["section"], mesh.shape["team"]
    chips = sections // CORES
    columns = 1
    while (2 * columns) ** 2 <= chips and chips % (2 * columns) == 0:
        columns *= 2
    spec = P("team", "section")
    return jax.shard_map(
        functools.partial(shards, sections, teams, columns),
        mesh=mesh, in_specs=(spec,) * 4, out_specs=spec, check_vma=False)
```

```python
import functools

import jax
import jax.numpy as jnp
from jax import lax
from jax.experimental import pallas as pl
from jax.experimental.pallas import tpu as pltpu
from jax.sharding import PartitionSpec as P

TILE = 128
NZ = 2
CORES = 2
MESH = pl.DeviceIdType.MESH


def kernel(sections, teams, columns, amps_ref, tm_ref, vm_ref, ints_ref, out_ref,
           mine, buf, v, texp, acc, part, got, load_sem, y_sem, send_sem, recv_sem, part_sem, got_sem):
    pieces, rows = mine.shape[0], texp.shape[0]
    panel = amps_ref.shape[1]
    row_tiles, tiles = rows // TILE, panel // TILE
    share = sections // teams
    levels = sections // (CORES * columns)
    step = CORES * columns
    width = min(share, step)
    depth, span = share // width, width // CORES
    s, t = lax.axis_index("section"), lax.axis_index("team")
    core, chip = lax.rem(s, CORES), lax.div(s, CORES)
    x, z = lax.rem(chip, columns), lax.div(chip, columns)
    group = lax.div(s, share)
    sibling = s + 1 - 2 * core
    first, offset = lax.div(t * share, step), lax.rem(t * share, step)

    def at(section, team):
        return {"section": section, "team": team}

    load = pltpu.make_async_copy(ints_ref, v, load_sem)
    load.start()

    barrier = pltpu.get_barrier_semaphore()

    def greet(section, team):
        pl.semaphore_signal(barrier, inc=1, device_id=at(section, team), device_id_type=MESH)

    greet(sibling, t)
    for d in range(1, columns):
        greet(s + CORES * (lax.rem(x + d, columns) - x), t)
    for d in range(1, teams):
        greet(s, lax.rem(t + d, teams))

    @pl.when(z > 0)
    def _():
        greet(s - step, t)

    @pl.when(z < levels - 1)
    def _():
        greet(s + step, t)

    partners = 1 + (columns - 1) + (teams - 1)
    partners = partners + jnp.where(z > 0, 1, 0) + jnp.where(z < levels - 1, 1, 0)

    def spread(table, i, c, j):
        row = table[i * tiles + c : i * tiles + c + 1, j * TILE : (j + 1) * TILE]
        return jnp.broadcast_to(row.astype(jnp.bfloat16), (TILE, TILE))

    shape = (mine.shape[1] - rows, NZ * TILE)
    table_row = lax.broadcasted_iota(jnp.int32, shape, 0)
    table_lane = lax.broadcasted_iota(jnp.int32, shape, 1)
    for h in range(pieces):
        hits = jnp.zeros(shape, jnp.float32)
        for i in range(row_tiles):
            before = jnp.int32(0)
            for c in range(tiles):
                one = tm_ref[h * row_tiles + i, c]
                for j in range(NZ):
                    hit = jnp.where(before == j, one, 0).astype(jnp.float32)
                    place = (table_row == i * tiles + c) & (table_lane >= j * TILE) & (table_lane < (j + 1) * TILE)
                    hits = jnp.where(place, hit, hits)
                before = before + one
        for i in range(row_tiles):
            r = (h * row_tiles + i) * TILE
            for j in range(NZ):
                total = None
                for c in range(tiles):
                    term = amps_ref[r : r + TILE, c * TILE : (c + 1) * TILE] * spread(hits, i, c, j)
                    total = term if total is None else total + term
                mine[h, i * TILE : (i + 1) * TILE, j * TILE : (j + 1) * TILE] = total
        mine[h, rows:, :] = hits.astype(jnp.bfloat16)

    def place_of(h, source, home):
        return (h * teams + source) * share + home

    def own(h):
        return place_of(h, t, lax.rem(s, share))

    @pl.when(group == t)
    def _():
        for h in range(pieces):
            buf[own(h)] = mine[h]

    pl.semaphore_wait(barrier, partners)

    def y_copy(h):
        return pltpu.make_async_remote_copy(
            src_ref=mine.at[h], dst_ref=buf.at[own(h)], send_sem=y_sem.at[h], recv_sem=recv_sem.at[own(h)],
            device_id=at(s, group), device_id_type=MESH)

    @pl.when(group != t)
    def _():
        for h in range(pieces):
            y_copy(h).start()

    phases = teams * pieces

    def slot(p, level, w):
        source = lax.rem(t + 1 + lax.div(p, pieces), teams)
        up, down = first + level, first + depth - 1 - level
        turn = first + lax.rem(z - first + level + depth, depth)
        row = jnp.where(z <= first, up, jnp.where(z >= first + depth - 1, down, turn))
        far = lax.rem(x + w, span)
        side = lax.rem(core + lax.div(w, span), CORES)
        home = row * step + offset + CORES * far + side
        u = home - t * share
        return source, u, place_of(lax.rem(p, pieces), source, u), home

    def relay(k, home, go):
        home_core, home_chip = lax.rem(home, CORES), lax.div(home, CORES)
        home_x, home_z = lax.rem(home_chip, columns), lax.div(home_chip, columns)
        straight = core == home_core
        column = straight & (x == home_x)

        def copy(kind, section):
            return pltpu.make_async_remote_copy(
                src_ref=buf.at[k], dst_ref=buf.at[k], send_sem=send_sem.at[kind, k], recv_sem=recv_sem.at[k],
                device_id=at(section, t), device_id_type=MESH)

        @pl.when(column & (z >= home_z) & (z < levels - 1))
        def _():
            go(copy(0, s + step))

        @pl.when(column & (z <= home_z) & (z > 0))
        def _():
            go(copy(1, s - step))

        for d in range(1, columns):
            @pl.when(column)
            def _():
                go(copy(2 + d, s + CORES * (lax.rem(x + d, columns) - x)))

        @pl.when(straight)
        def _():
            go(copy(2, sibling))

    def arrive(k, home, source):
        @pl.when((s != home) | (source != t))
        def _():
            pltpu.make_async_remote_copy(
                src_ref=buf.at[k], dst_ref=buf.at[k], send_sem=send_sem.at[2, k], recv_sem=recv_sem.at[k],
                device_id=at(sibling, t), device_id_type=MESH).wait_recv()

    def pass_on(p, level, w):
        source, _, k, home = slot(p, level, w)
        arrive(k, home, source)
        relay(k, home, lambda copy: copy.start())

    @pl.when(group == t)
    def _():
        for h in range(pieces):
            relay(own(h), s, lambda copy: copy.start())

    def part_copy(p):
        d, h = p // pieces + 1, p % pieces
        there = (teams - d - 1) * pieces + h
        return pltpu.make_async_remote_copy(
            src_ref=part.at[p], dst_ref=got.at[there], send_sem=part_sem.at[p],
            recv_sem=got_sem.at[there], device_id=at(s, lax.rem(t + d, teams)), device_id_type=MESH)

    def columns_of(p):
        for level in range(1 if p >= phases - pieces else 0, depth):
            pass_on(p, level, 0)

    def rest_of(p):
        for level in range(depth):
            for w in range(1, span):
                pass_on(p, level, w)

    def compute(p):
        acc[...] = jnp.zeros_like(acc)

        @pl.loop(0, share)
        def _(n):
            level, w = lax.div(n, width), lax.rem(n, width)
            source, u, k, home = slot(p, level, w)

            @pl.when(w >= span)
            def _():
                arrive(k, home, source)

            table = buf[k, rows:, :].astype(jnp.float32)
            for i in range(row_tiles):
                for c in range(tiles):
                    tile = None
                    for j in range(NZ):
                        term = buf[k, i * TILE : (i + 1) * TILE, j * TILE : (j + 1) * TILE] * spread(table, i, c, j)
                        tile = term if tile is None else tile + term
                    texp[i * TILE : (i + 1) * TILE, c * TILE : (c + 1) * TILE] = tile
            here = pl.ds(pl.multiple_of(u * panel, panel), panel)
            acc[...] += jnp.dot(texp[...], v[here, :], preferred_element_type=jnp.float32)

    for p in range(phases - pieces, phases):
        source, _, k, home = slot(p, 0, 0)

        @pl.when(s != home)
        def _():
            pass_on(p, 0, 0)

    columns_of(0)
    load.wait()

    @pl.loop(0, v.shape[0] // TILE)
    def _(k):
        here = pl.ds(pl.multiple_of(k * TILE, TILE), TILE)
        for c in range(v.shape[1] // TILE):
            lanes = slice(c * TILE, (c + 1) * TILE)
            v[here, lanes] = v[here, lanes] * jnp.full((TILE, TILE), vm_ref[k, c].astype(jnp.float32)).astype(jnp.bfloat16)

    for p in range(phases):
        if p + 1 < phases:
            columns_of(p + 1)
        rest_of(p)
        compute(p)
        if p < phases - pieces:
            part[p] = acc[...]
            part_copy(p).start()
        else:
            h = p - (phases - pieces)
            for d in range(1, teams):
                there = (d - 1) * pieces + h
                part_copy((teams - d - 1) * pieces + h).wait_recv()
                acc[...] += got[there]
            out_ref[h * rows : (h + 1) * rows, :] = acc[...].astype(out_ref.dtype)

    @pl.when(group != t)
    def _():
        for h in range(pieces):
            y_copy(h).wait_send()

    @pl.loop(0, phases * share)
    def _(n):
        p, n = lax.div(n, share), lax.rem(n, share)
        _, _, k, home = slot(p, lax.div(n, width), lax.rem(n, width))
        relay(k, home, lambda copy: copy.wait_send())

    for p in range(phases - pieces):
        part_copy(p).wait_send()


def shards(sections, teams, columns, amps, t_mask, ints, v_mask):
    rows, panel = amps.shape
    depth, ab_cols = ints.shape
    row_tiles = rows // TILE
    pieces = 2 if row_tiles % 2 == 0 else 1
    piece = rows // pieces
    table = t_mask.shape[0] * t_mask.shape[1] // pieces
    message = (piece + -(-table // 16) * 16, NZ * TILE)
    slots, parts = pieces * sections, pieces * (teams - 1)
    smem = pl.BlockSpec(memory_space=pltpu.SMEM)
    vmem = pl.BlockSpec(memory_space=pltpu.VMEM)
    return pl.pallas_call(
        functools.partial(kernel, sections, teams, columns),
        out_shape=jax.ShapeDtypeStruct((rows, ab_cols), jnp.bfloat16),
        in_specs=[vmem, smem, smem, pl.BlockSpec(memory_space=pl.ANY)],
        out_specs=vmem,
        scratch_shapes=[
            pltpu.VMEM((pieces, *message), jnp.bfloat16),
            pltpu.VMEM((slots, *message), jnp.bfloat16),
            pltpu.VMEM((depth, ab_cols), jnp.bfloat16),
            pltpu.VMEM((piece, panel), jnp.bfloat16),
            pltpu.VMEM((piece, ab_cols), jnp.float32),
            pltpu.VMEM((parts, piece, ab_cols), jnp.float32),
            pltpu.VMEM((parts, piece, ab_cols), jnp.float32),
            pltpu.SemaphoreType.DMA,
            pltpu.SemaphoreType.DMA((pieces,)),
            pltpu.SemaphoreType.DMA((2 + columns, slots)),
            pltpu.SemaphoreType.DMA((slots,)),
            pltpu.SemaphoreType.DMA((parts,)),
            pltpu.SemaphoreType.DMA((parts,)),
        ],
        compiler_params=pltpu.CompilerParams(
            collective_id=0, has_side_effects=True, vmem_limit_bytes=60 * 2**20
        ),
        cost_estimate=pl.CostEstimate(
            flops=2 * teams * rows * depth * ab_cols, bytes_accessed=2 * depth * ab_cols, transcendentals=0
        ),
    )(amps, t_mask, v_mask, ints)


def solution(mesh):
    sections, teams = mesh.shape["section"], mesh.shape["team"]
    chips = sections // CORES
    columns = 1
    while (2 * columns) ** 2 <= chips and chips % (2 * columns) == 0:
        columns *= 2
    spec = P("team", "section")
    return jax.shard_map(
        functools.partial(shards, sections, teams, columns),
        mesh=mesh, in_specs=(spec,) * 4, out_specs=spec, check_vma=False)
```

```python
import functools

import jax
import jax.numpy as jnp
from jax import lax
from jax.experimental import pallas as pl
from jax.experimental.pallas import tpu as pltpu
from jax.sharding import PartitionSpec as P

TILE = 128
NZ = 2
CORES = 2
MESH = pl.DeviceIdType.MESH


def kernel(sections, teams, columns, amps_ref, tm_ref, vm_ref, ints_ref, out_ref,
           mine, buf, v, texp, acc, part, got, load_sem, y_sem, send_sem, recv_sem, part_sem, got_sem):
    pieces, rows = mine.shape[0], texp.shape[0]
    panel = amps_ref.shape[1]
    row_tiles, tiles = rows // TILE, panel // TILE
    share = sections // teams
    levels = sections // (CORES * columns)
    step = CORES * columns
    width = min(share, step)
    depth, span = share // width, width // CORES
    s, t = lax.axis_index("section"), lax.axis_index("team")
    core, chip = lax.rem(s, CORES), lax.div(s, CORES)
    x, z = lax.rem(chip, columns), lax.div(chip, columns)
    group = lax.div(s, share)
    sibling = s + 1 - 2 * core
    first, offset = lax.div(t * share, step), lax.rem(t * share, step)

    def at(section, team):
        return {"section": section, "team": team}

    load = pltpu.make_async_copy(ints_ref, v, load_sem)
    load.start()

    barrier = pltpu.get_barrier_semaphore()

    def greet(section, team):
        pl.semaphore_signal(barrier, inc=1, device_id=at(section, team), device_id_type=MESH)

    greet(sibling, t)
    for d in range(1, columns):
        greet(s + CORES * (lax.rem(x + d, columns) - x), t)
    for d in range(1, teams):
        greet(s, lax.rem(t + d, teams))

    @pl.when(z > 0)
    def _():
        greet(s - step, t)

    @pl.when(z < levels - 1)
    def _():
        greet(s + step, t)

    partners = 1 + (columns - 1) + (teams - 1)
    partners = partners + jnp.where(z > 0, 1, 0) + jnp.where(z < levels - 1, 1, 0)

    def spread(table, i, c, j):
        row = table[i * tiles + c : i * tiles + c + 1, j * TILE : (j + 1) * TILE]
        return jnp.broadcast_to(row.astype(jnp.bfloat16), (TILE, TILE))

    shape = (mine.shape[1] - rows, NZ * TILE)
    table_row = lax.broadcasted_iota(jnp.int32, shape, 0)
    table_lane = lax.broadcasted_iota(jnp.int32, shape, 1)
    for h in range(pieces):
        hits = jnp.zeros(shape, jnp.float32)
        for i in range(row_tiles):
            before = jnp.int32(0)
            for c in range(tiles):
                one = tm_ref[h * row_tiles + i, c]
                for j in range(NZ):
                    hit = jnp.where(before == j, one, 0).astype(jnp.float32)
                    place = (table_row == i * tiles + c) & (table_lane >= j * TILE) & (table_lane < (j + 1) * TILE)
                    hits = jnp.where(place, hit, hits)
                before = before + one
        for i in range(row_tiles):
            r = (h * row_tiles + i) * TILE
            for j in range(NZ):
                total = None
                for c in range(tiles):
                    term = amps_ref[r : r + TILE, c * TILE : (c + 1) * TILE] * spread(hits, i, c, j)
                    total = term if total is None else total + term
                mine[h, i * TILE : (i + 1) * TILE, j * TILE : (j + 1) * TILE] = total
        mine[h, rows:, :] = hits.astype(jnp.bfloat16)

    def place_of(h, source, home):
        return (h * teams + source) * share + home

    def own(h):
        return place_of(h, t, lax.rem(s, share))

    @pl.when(group == t)
    def _():
        for h in range(pieces):
            buf[own(h)] = mine[h]

    pl.semaphore_wait(barrier, partners)

    def y_copy(h):
        return pltpu.make_async_remote_copy(
            src_ref=mine.at[h], dst_ref=buf.at[own(h)], send_sem=y_sem.at[h], recv_sem=recv_sem.at[own(h)],
            device_id=at(s, group), device_id_type=MESH)

    @pl.when(group != t)
    def _():
        for h in range(pieces):
            y_copy(h).start()

    phases = teams * pieces

    def slot(p, level, w):
        source = lax.rem(t + 1 + lax.div(p, pieces), teams)
        up, down = first + level, first + depth - 1 - level
        turn = first + lax.rem(z - first + level + depth, depth)
        row = jnp.where(z <= first, up, jnp.where(z >= first + depth - 1, down, turn))
        far = lax.rem(x + w, span)
        side = lax.rem(core + lax.div(w, span), CORES)
        home = row * step + offset + CORES * far + side
        u = home - t * share
        return source, u, place_of(lax.rem(p, pieces), source, u), home

    def relay(k, home, go):
        home_core, home_chip = lax.rem(home, CORES), lax.div(home, CORES)
        home_x, home_z = lax.rem(home_chip, columns), lax.div(home_chip, columns)
        straight = core == home_core
        column = straight & (x == home_x)

        def copy(kind, section):
            return pltpu.make_async_remote_copy(
                src_ref=buf.at[k], dst_ref=buf.at[k], send_sem=send_sem.at[kind, k], recv_sem=recv_sem.at[k],
                device_id=at(section, t), device_id_type=MESH)

        @pl.when(column & (z >= home_z) & (z < levels - 1))
        def _():
            go(copy(0, s + step))

        @pl.when(column & (z <= home_z) & (z > 0))
        def _():
            go(copy(1, s - step))

        for d in range(1, columns):
            @pl.when(column)
            def _():
                go(copy(2 + d, s + CORES * (lax.rem(x + d, columns) - x)))

        @pl.when(straight)
        def _():
            go(copy(2, sibling))

    def arrive(k, home, source):
        @pl.when((s != home) | (source != t))
        def _():
            pltpu.make_async_remote_copy(
                src_ref=buf.at[k], dst_ref=buf.at[k], send_sem=send_sem.at[2, k], recv_sem=recv_sem.at[k],
                device_id=at(sibling, t), device_id_type=MESH).wait_recv()

    def pass_on(p, level, w):
        source, _, k, home = slot(p, level, w)
        arrive(k, home, source)
        relay(k, home, lambda copy: copy.start())

    @pl.when(group == t)
    def _():
        for h in range(pieces):
            relay(own(h), s, lambda copy: copy.start())

    def part_copy(p):
        d, h = p // pieces + 1, p % pieces
        there = (teams - d - 1) * pieces + h
        return pltpu.make_async_remote_copy(
            src_ref=part.at[p], dst_ref=got.at[there], send_sem=part_sem.at[p],
            recv_sem=got_sem.at[there], device_id=at(s, lax.rem(t + d, teams)), device_id_type=MESH)

    def columns_of(p):
        for level in range(1 if p >= phases - pieces else 0, depth):
            pass_on(p, level, 0)

    def rest_of(p):
        for level in range(depth):
            for w in range(1, span):
                pass_on(p, level, w)

    def compute(p):
        acc[...] = jnp.zeros_like(acc)

        @pl.loop(0, share)
        def _(n):
            level, w = lax.div(n, width), lax.rem(n, width)
            source, u, k, home = slot(p, level, w)

            @pl.when(w >= span)
            def _():
                arrive(k, home, source)

            table = buf[k, rows:, :].astype(jnp.float32)
            for i in range(row_tiles):
                for c in range(tiles):
                    tile = None
                    for j in range(NZ):
                        term = buf[k, i * TILE : (i + 1) * TILE, j * TILE : (j + 1) * TILE] * spread(table, i, c, j)
                        tile = term if tile is None else tile + term
                    texp[i * TILE : (i + 1) * TILE, c * TILE : (c + 1) * TILE] = tile
            here = pl.ds(pl.multiple_of(u * panel, panel), panel)
            acc[...] += jnp.dot(texp[...], v[here, :], preferred_element_type=jnp.float32)

    for p in range(phases - pieces, phases):
        source, _, k, home = slot(p, 0, 0)

        @pl.when(s != home)
        def _():
            pass_on(p, 0, 0)

    columns_of(0)
    load.wait()

    @pl.loop(0, v.shape[0] // TILE)
    def _(k):
        here = pl.ds(pl.multiple_of(k * TILE, TILE), TILE)
        for c in range(v.shape[1] // TILE):
            lanes = slice(c * TILE, (c + 1) * TILE)
            v[here, lanes] = v[here, lanes] * jnp.full((TILE, TILE), vm_ref[k, c].astype(jnp.float32)).astype(jnp.bfloat16)

    for p in range(phases):
        rest_of(p)
        if p + 1 < phases:
            columns_of(p + 1)
        compute(p)
        if p < phases - pieces:
            part[p] = acc[...]
            part_copy(p).start()
        else:
            h = p - (phases - pieces)
            for d in range(1, teams):
                there = (d - 1) * pieces + h
                part_copy((teams - d - 1) * pieces + h).wait_recv()
                acc[...] += got[there]
            out_ref[h * rows : (h + 1) * rows, :] = acc[...].astype(out_ref.dtype)

    @pl.when(group != t)
    def _():
        for h in range(pieces):
            y_copy(h).wait_send()

    @pl.loop(0, phases * share)
    def _(n):
        p, n = lax.div(n, share), lax.rem(n, share)
        _, _, k, home = slot(p, lax.div(n, width), lax.rem(n, width))
        relay(k, home, lambda copy: copy.wait_send())

    for p in range(phases - pieces):
        part_copy(p).wait_send()


def shards(sections, teams, columns, amps, t_mask, ints, v_mask):
    rows, panel = amps.shape
    depth, ab_cols = ints.shape
    row_tiles = rows // TILE
    pieces = 2 if row_tiles % 2 == 0 else 1
    piece = rows // pieces
    table = t_mask.shape[0] * t_mask.shape[1] // pieces
    message = (piece + -(-table // 16) * 16, NZ * TILE)
    slots, parts = pieces * sections, pieces * (teams - 1)
    smem = pl.BlockSpec(memory_space=pltpu.SMEM)
    vmem = pl.BlockSpec(memory_space=pltpu.VMEM)
    return pl.pallas_call(
        functools.partial(kernel, sections, teams, columns),
        out_shape=jax.ShapeDtypeStruct((rows, ab_cols), jnp.bfloat16),
        in_specs=[vmem, smem, smem, pl.BlockSpec(memory_space=pl.ANY)],
        out_specs=vmem,
        scratch_shapes=[
            pltpu.VMEM((pieces, *message), jnp.bfloat16),
            pltpu.VMEM((slots, *message), jnp.bfloat16),
            pltpu.VMEM((depth, ab_cols), jnp.bfloat16),
            pltpu.VMEM((piece, panel), jnp.bfloat16),
            pltpu.VMEM((piece, ab_cols), jnp.float32),
            pltpu.VMEM((parts, piece, ab_cols), jnp.float32),
            pltpu.VMEM((parts, piece, ab_cols), jnp.float32),
            pltpu.SemaphoreType.DMA,
            pltpu.SemaphoreType.DMA((pieces,)),
            pltpu.SemaphoreType.DMA((2 + columns, slots)),
            pltpu.SemaphoreType.DMA((slots,)),
            pltpu.SemaphoreType.DMA((parts,)),
            pltpu.SemaphoreType.DMA((parts,)),
        ],
        compiler_params=pltpu.CompilerParams(
            collective_id=0, has_side_effects=True, vmem_limit_bytes=60 * 2**20
        ),
        cost_estimate=pl.CostEstimate(
            flops=2 * teams * rows * depth * ab_cols, bytes_accessed=2 * depth * ab_cols, transcendentals=0
        ),
    )(amps, t_mask, v_mask, ints)


def solution(mesh):
    sections, teams = mesh.shape["section"], mesh.shape["team"]
    chips = sections // CORES
    columns = 1
    while (2 * columns) ** 2 <= chips and chips % (2 * columns) == 0:
        columns *= 2
    spec = P("team", "section")
    return jax.shard_map(
        functools.partial(shards, sections, teams, columns),
        mesh=mesh, in_specs=(spec,) * 4, out_specs=spec, check_vma=False)
```
